32 devices in a mesh: member: 2 (over y), band: 4 (over z), face: 2 (over x), rep: 2 (over core).
Axes of the slice: x: 2, y: 2, z: 4, core: 2. Of those that a mesh axis runs over, the one named last changes fastest.
Arguments:
- grid_latent: bfloat16 [32, 192, 512], P(('member', 'band'), ('face', 'rep')), parts along dimension 0, may hold values from -6 to 6
- mesh_latent: bfloat16 [2048, 512], P(('member', 'band', 'face', 'rep')), parts along dimension 0, may hold values from -6 to 6
- w_grid_send: bfloat16 [512, 512], replicated, may hold values from -0.25 to 0.25
- w_mesh_recv: bfloat16 [512, 512], replicated, may hold values from -0.25 to 0.25
- w_g2m_geom: bfloat16 [4, 512], replicated, may hold values from -3 to 3
- w_g2m_out: bfloat16 [512, 512], replicated, may hold values from -0.25 to 0.25
- g2m_gain: float32 [512], replicated, may hold values from 0.5 to 1.5
- w_node_mesh: bfloat16 [512, 512], replicated, may hold values from -0.25 to 0.25
- w_node_agg: bfloat16 [512, 512], replicated, may hold values from -0.25 to 0.25
- w_node_out: bfloat16 [512, 512], replicated, may hold values from -0.25 to 0.25
- node_gain: float32 [512], replicated, may hold values from 0.5 to 1.5
- w_proc_send: bfloat16 [512, 512], replicated, may hold values from -0.25 to 0.25
- w_proc_recv: bfloat16 [512, 512], replicated, may hold values from -0.25 to 0.25
- w_proc_geom: bfloat16 [4, 512], replicated, may hold values from -3 to 3
- w_proc_out: bfloat16 [512, 512], replicated, may hold values from -0.25 to 0.25
- proc_gain: float32 [512], replicated, may hold values from 0.5 to 1.5
- g2m_sender: int32 [32768], P(('band', 'face', 'rep')), may hold values from 0 to 3071, as said below
- g2m_receiver: int32 [32768], P(('band', 'face', 'rep')), may hold values from 0 to 63
- g2m_geom: bfloat16 [4, 32768], P(None, ('band', 'face', 'rep')), may hold values from -6 to 6
- g2m_count: int32 [16], P(('band', 'face', 'rep')), may hold values from 512 to 2048, as said below
- mesh_receiver: int32 [16384], P(('band', 'face', 'rep')), may hold values from 0 to 63
- mesh_slot: int32 [16384], P(('band', 'face', 'rep')), may hold values from 0 to 15
- send_rows: int32 [256], P(('band', 'face', 'rep')), may hold values from 0 to 63, as said below
- mesh_geom: bfloat16 [4, 16384], P(None, ('band', 'face', 'rep')), may hold values from -6 to 6
- mesh_count: int32 [16], P(('band', 'face', 'rep')), may hold values from 256 to 1024, as said below
Outputs:
- mesh_encoded: bfloat16 [2048, 512], P(('member', 'band', 'face', 'rep')), parts along dimension 0
- mesh_messages: bfloat16 [2048, 512], P(('member', 'band', 'face', 'rep')), parts along dimension 0
The draws below stay inside these ranges and needn't reach their ends.
There are 2 independent parts, one for each index of `member`. The reference program is written for one: setup_inputs(seed, part) draws one part's arguments, and reference() takes and returns one part's arrays. A program takes and returns all parts, laid end to end along the dimension named above; an argument that names none is the same for every part. Nothing has to cross between parts.
Inputs may be any that keep to these rules, and one draw needn't show every extreme that they name: `g2m_sender`: the grid node of a slot of device d lies in d's longitude columns and within 2 latitude rows of d's rows (clipped at the poles). `g2m_count`: devices of the first and last band have exactly 2048 live slots. `mesh_count`: devices of the first and last band have exactly 1024 live slots. `send_rows`: the 2 rows that one device lists for one peer are distinct.
All inputs are finite; a program needn't handle non-finite values.
Results may differ from the reference program's by a relative error of at most 0.0085.
Values may be sent and summed in bfloat16 or wider, within the bound.
A program may use at most 64 MiB of HBM per device.

```python
import jax
import jax.numpy as jnp
from jax import lax

D = 512
LAT_DEV = 4
LON_DEV = 48
MESH_DEV = 64
G_CAP = 2048
M_CAP = 1024
SLOT = 2
RIM = 2
REPS = 2
PEERS = 8
DEV_PART = 16
LAT = 16
LON = 192
MESH = 1024
G_EDGES = 32768
M_EDGES = 16384
N_BAND = 4


def count_law(key, capacity):
    band_index = jnp.arange(DEV_PART, dtype=jnp.int32) // (DEV_PART // N_BAND)
    polar_band = (band_index == 0) | (band_index == N_BAND - 1)
    inner_count = jax.random.randint(key, (DEV_PART,), capacity // 4, capacity // 2 + 1, dtype=jnp.int32)
    return jnp.where(polar_band, capacity, inner_count).astype(jnp.int32)


def draw_g2m_count(key, part):
    key = jax.random.fold_in(key, 11)
    return count_law(key, G_CAP)


def draw_mesh_count(key, part):
    key = jax.random.fold_in(key, 12)
    return count_law(key, M_CAP)


def draw_g2m_sender(key, part):
    key = jax.random.fold_in(key, 13)
    lat_key, lon_key = jax.random.split(key)
    slot_index = jnp.arange(G_EDGES, dtype=jnp.int32)
    device = slot_index // G_CAP
    within = slot_index % G_CAP
    band_index = device // (DEV_PART // N_BAND)
    column = device % (DEV_PART // N_BAND)
    lat_offset = jax.random.randint(lat_key, (G_EDGES,), 0, LAT_DEV + 2 * RIM, dtype=jnp.int32)
    lon_offset = jax.random.randint(lon_key, (G_EDGES,), 0, LON_DEV, dtype=jnp.int32)
    lat_offset = jnp.where(within == 0, LAT_DEV + 2 * RIM - 1, jnp.where(within == 1, 0, lat_offset))
    lon_offset = jnp.where(within == 0, LON_DEV - 1, jnp.where(within == 1, 0, lon_offset))
    latitude = jnp.clip(band_index * LAT_DEV - RIM + lat_offset, 0, LAT - 1)
    longitude = column * LON_DEV + lon_offset
    return (latitude * LON + longitude).astype(jnp.int32)


def draw_send_rows(key, part):
    key = jax.random.fold_in(key, 14)
    scores = jax.random.randint(key, (DEV_PART, PEERS, MESH_DEV), 0, 1 << 20, dtype=jnp.int32)
    scores = scores * MESH_DEV + jnp.arange(MESH_DEV, dtype=jnp.int32)
    ranked = jnp.argsort(scores, axis=-1)[:, :, :SLOT]
    return ranked.reshape(DEV_PART * PEERS * SLOT).astype(jnp.int32)


def set_ends(entries, stream_key, least, high):
    shape = entries.shape
    place = [jax.random.randint(jax.random.fold_in(stream_key, axis), (), 0, shape[axis]) for axis in range(len(shape))]
    entries = entries.at[tuple(place)].set(least)
    longest = shape.index(max(shape))
    place[longest] = (place[longest] + 1) % shape[longest]
    return entries.at[tuple(place)].set(high)


def level_of(own_key, shape, cuts, least, high):
    def one(dim, shards_of):
        heights = jax.random.uniform(jax.random.fold_in(jax.random.fold_in(own_key, 6), dim), (shards_of,), jnp.float32, least / len(cuts), high / len(cuts))
        return jnp.repeat(jnp.exp(heights), shape[dim] // shards_of).reshape((-1,) + (1,) * (len(shape) - dim - 1))

    factor_of = one(*cuts[0])
    for cut in cuts[1:]:
        factor_of = factor_of * one(*cut)
    return factor_of


def bell_draw(rng, shape, scale, bound, cuts=(), kind=jnp.bfloat16):
    array = jax.random.normal(rng, shape, jnp.float32) * scale
    if len(cuts) > 0:
        array = level_of(rng, shape, cuts, -0.22, 0.18) * array
    return jnp.clip(array, min=-bound, max=bound).astype(kind)


def setup_inputs(seed: int = 0, part: int = 0) -> dict:
    arg_keys = jax.random.split(jax.random.key(seed), 26)
    own_keys = jax.random.split(jax.random.fold_in(arg_keys[25], part), 26)
    grid_latent = bell_draw(own_keys[0], (LAT, LON, D), 1.0, 6.0, ((0, 4), (1, 4)))
    mesh_latent = bell_draw(own_keys[1], (MESH, D), 1.0, 6.0, ((0, 16),))
    w_grid_send = bell_draw(arg_keys[2], (D, D), D ** -0.5, 0.25)
    w_mesh_recv = bell_draw(arg_keys[3], (D, D), D ** -0.5, 0.25)
    w_g2m_geom = bell_draw(arg_keys[4], (4, D), 4 ** -0.5, 3.0)
    w_g2m_out = bell_draw(arg_keys[5], (D, D), D ** -0.5, 0.25)
    g2m_gain = jnp.clip(1.0 + 0.1 * jax.random.normal(arg_keys[6], (D,), jnp.float32), 0.5, 1.5)
    w_node_mesh = bell_draw(arg_keys[7], (D, D), D ** -0.5, 0.25)
    w_node_agg = bell_draw(arg_keys[8], (D, D), D ** -0.5, 0.25)
    w_node_out = bell_draw(arg_keys[9], (D, D), D ** -0.5, 0.25)
    node_gain = jnp.clip(1.0 + 0.1 * jax.random.normal(arg_keys[10], (D,), jnp.float32), 0.5, 1.5)
    w_proc_send = bell_draw(arg_keys[11], (D, D), D ** -0.5, 0.25)
    w_proc_recv = bell_draw(arg_keys[12], (D, D), D ** -0.5, 0.25)
    w_proc_geom = bell_draw(arg_keys[13], (4, D), 4 ** -0.5, 3.0)
    w_proc_out = bell_draw(arg_keys[14], (D, D), D ** -0.5, 0.25)
    proc_gain = jnp.clip(1.0 + 0.1 * jax.random.normal(arg_keys[15], (D,), jnp.float32), 0.5, 1.5)
    g2m_sender = draw_g2m_sender(jax.random.fold_in(arg_keys[25], 71), part)
    g2m_receiver = set_ends(jax.random.randint(arg_keys[17], (G_EDGES,), 0, MESH_DEV), jax.random.fold_in(arg_keys[17], 1), 0, MESH_DEV - 1).astype(jnp.int32)
    g2m_geom = bell_draw(arg_keys[18], (4, G_EDGES), 1.0, 6.0, ((1, 16),))
    g2m_count = draw_g2m_count(jax.random.fold_in(arg_keys[25], 71), part)
    mesh_receiver = set_ends(jax.random.randint(arg_keys[20], (M_EDGES,), 0, MESH_DEV), jax.random.fold_in(arg_keys[20], 1), 0, MESH_DEV - 1).astype(jnp.int32)
    mesh_slot = set_ends(jax.random.randint(arg_keys[21], (M_EDGES,), 0, PEERS * SLOT), jax.random.fold_in(arg_keys[21], 1), 0, (PEERS * SLOT) - 1).astype(jnp.int32)
    send_rows = draw_send_rows(jax.random.fold_in(arg_keys[25], 71), part)
    mesh_geom = bell_draw(arg_keys[23], (4, M_EDGES), 1.0, 6.0, ((1, 16),))
    mesh_count = draw_mesh_count(jax.random.fold_in(arg_keys[25], 71), part)
    return dict(grid_latent=grid_latent, mesh_latent=mesh_latent, w_grid_send=w_grid_send, w_mesh_recv=w_mesh_recv, w_g2m_geom=w_g2m_geom, w_g2m_out=w_g2m_out, g2m_gain=g2m_gain, w_node_mesh=w_node_mesh, w_node_agg=w_node_agg, w_node_out=w_node_out, node_gain=node_gain, w_proc_send=w_proc_send, w_proc_recv=w_proc_recv, w_proc_geom=w_proc_geom, w_proc_out=w_proc_out, proc_gain=proc_gain, g2m_sender=g2m_sender, g2m_receiver=g2m_receiver, g2m_geom=g2m_geom, g2m_count=g2m_count, mesh_receiver=mesh_receiver, mesh_slot=mesh_slot, send_rows=send_rows, mesh_geom=mesh_geom, mesh_count=mesh_count)


EPSILON = 1e-05

def layer_norm(values, scale_gain):
    center = values - lax.optimization_barrier(jnp.mean(values, axis=-1, keepdims=True))
    spread = lax.optimization_barrier(jnp.mean(center * center, axis=-1, keepdims=True))
    return center * lax.rsqrt(spread + EPSILON) * scale_gain

def project(row_block, weight):
    return jnp.dot(row_block, weight, preferred_element_type=jnp.float32).astype(jnp.bfloat16)

def edge_terms(sender_rows, receiver_rows, geometry, w_geom, w_out, scale_gain, live_mask, receivers, node_count):
    mixed_sum = sender_rows.astype(jnp.float32) + receiver_rows.astype(jnp.float32)
    mixed_sum = mixed_sum + jnp.dot(geometry.T, w_geom, preferred_element_type=jnp.float32)
    hidden = jax.nn.silu(mixed_sum).astype(jnp.bfloat16)
    output = jnp.dot(hidden, w_out, preferred_element_type=jnp.float32)
    message = jnp.where(live_mask[:, None], layer_norm(output, scale_gain), 0.0).astype(jnp.bfloat16)
    onehot = (receivers[None, :] == jnp.arange(node_count, dtype=jnp.int32)[:, None]).astype(jnp.bfloat16)
    return jnp.dot(onehot, message, preferred_element_type=jnp.float32)

def reference(grid_latent, mesh_latent, w_grid_send, w_mesh_recv, w_g2m_geom, w_g2m_out, g2m_gain, w_node_mesh, w_node_agg, w_node_out, node_gain, w_proc_send, w_proc_recv, w_proc_geom, w_proc_out, proc_gain, g2m_sender, g2m_receiver, g2m_geom, g2m_count, mesh_receiver, mesh_slot, send_rows, mesh_geom, mesh_count):
    width = grid_latent.shape[-1]
    grid_proj = project(grid_latent.reshape(LAT * LON, width), w_grid_send)
    mesh_proj = project(mesh_latent, w_mesh_recv)

    def encode_block(device):
        start = (device * G_CAP).astype(jnp.int32)
        senders = lax.dynamic_slice_in_dim(g2m_sender, start, G_CAP)
        receivers = lax.dynamic_slice_in_dim(g2m_receiver, start, G_CAP)
        geometry = lax.dynamic_slice_in_dim(g2m_geom, start, G_CAP, 1)
        live_mask = jnp.arange(G_CAP, dtype=jnp.int32) < g2m_count[device]
        row_table = lax.dynamic_slice_in_dim(mesh_proj, (device * MESH_DEV).astype(jnp.int32), MESH_DEV)
        return edge_terms(grid_proj[senders], row_table[receivers], geometry, w_g2m_geom, w_g2m_out, g2m_gain, live_mask, receivers, MESH_DEV)
    devices = jnp.arange(DEV_PART, dtype=jnp.int32)
    g2m_sum = lax.map(encode_block, devices).reshape(MESH, width).astype(jnp.bfloat16)
    node_input = jnp.dot(mesh_latent, w_node_mesh, preferred_element_type=jnp.float32)
    node_input = node_input + jnp.dot(g2m_sum, w_node_agg, preferred_element_type=jnp.float32)
    node_hidden = jax.nn.silu(node_input).astype(jnp.bfloat16)
    update = layer_norm(jnp.dot(node_hidden, w_node_out, preferred_element_type=jnp.float32), node_gain)
    mesh_encoded = (mesh_latent.astype(jnp.float32) + update).astype(jnp.bfloat16)
    send_proj = project(mesh_encoded, w_proc_send)
    recv_proj = project(mesh_encoded, w_proc_recv)
    send_table = send_rows.reshape(DEV_PART, PEERS, SLOT)

    def process_block(device):
        start = (device * M_CAP).astype(jnp.int32)
        slot_ids = lax.dynamic_slice_in_dim(mesh_slot, start, M_CAP)
        receivers = lax.dynamic_slice_in_dim(mesh_receiver, start, M_CAP)
        geometry = lax.dynamic_slice_in_dim(mesh_geom, start, M_CAP, 1)
        live_mask = jnp.arange(M_CAP, dtype=jnp.int32) < mesh_count[device]
        source = (slot_ids // SLOT * REPS + device % REPS).astype(jnp.int32)
        row_index = send_table[source, device // REPS, slot_ids % SLOT]
        senders = (source * MESH_DEV + row_index).astype(jnp.int32)
        row_table = lax.dynamic_slice_in_dim(recv_proj, (device * MESH_DEV).astype(jnp.int32), MESH_DEV)
        return edge_terms(send_proj[senders], row_table[receivers], geometry, w_proc_geom, w_proc_out, proc_gain, live_mask, receivers, MESH_DEV)
    mesh_messages = lax.map(process_block, devices).reshape(MESH, width).astype(jnp.bfloat16)
    return (mesh_encoded, mesh_messages)
```

```python
import functools

import jax
import jax.numpy as jnp
from jax import lax
from jax.experimental import pallas as pl
from jax.experimental.pallas import tpu as pltpu
from jax.sharding import PartitionSpec as P

RIM = 2
EPSILON = 1e-05
LANES = 128
TILE = 256
BF = jnp.bfloat16
F32 = jnp.float32

GRID_SEND, MESH_RECV, G2M_OUT, NODE_MESH, NODE_AGG, NODE_OUT, PROC_SEND, PROC_RECV, PROC_OUT = range(9)


def dot(a, b, contract=((1,), (0,))):
    return lax.dot_general(a, b, (contract, ((), ())), preferred_element_type=F32)


def silu(v):
    half = 0.5 * v
    return half + half * jnp.tanh(half)


def normalized(y, axis):
    scale = 1.0 / y.shape[axis]
    center = y - jnp.sum(y, axis=axis, keepdims=True) * scale
    spread = jnp.sum(center * center, axis=axis, keepdims=True) * scale
    return center * lax.rsqrt(spread + EPSILON)


def hot(index_row, rows):
    edges = index_row.shape[1]
    return jnp.where(lax.broadcasted_iota(jnp.int32, (rows, edges), 0) == index_row, 1.0, 0.0).astype(BF)


def edge_sum(table_t, out_t, hot_ref, receiver_row, nodes, edges):
    total = None
    for start in range(0, edges, TILE):
        cols = pl.ds(start, TILE)
        hidden = silu(dot(table_t[...], hot_ref[:, cols])).astype(BF)
        message = normalized(dot(out_t[...], hidden), 0).astype(BF)
        part = dot(hot_ref[pl.ds(receiver_row, nodes), cols], message, ((1,), (1,)))
        total = part if total is None else total + part
    return total


def kernel(
    dims,
    grid_hbm, mesh_hbm, w0, w1, w2, w3, w4, w5, w6, w7, w8,
    wgg, wpg, g2m_gain, node_gain, proc_gain,
    g2m_sender, g2m_receiver, g2m_geom, mesh_receiver, mesh_slot, send_rows, mesh_geom,
    g2m_count, mesh_count,
    enc_out, msg_out,
    grid_v, mesh_v, w_v, table, table_t, out_t, hot_g, hot_m, table_m, table_mt, out_mt, send_buf, recv_buf,
    load_sem, halo_send, halo_recv, row_send, row_recv,
):
    bands, faces, reps, lat_rows, lon_cols, full_lon = dims
    own, width = grid_v.shape
    nodes = mesh_v.shape[0]
    rim = RIM * lon_cols
    g_edges, m_edges = hot_g.shape[1], hot_m.shape[1]
    listed = send_rows.shape[1]
    peers = bands * faces
    slot_rows = send_buf.shape[0] // peers
    chunks = width // LANES
    band, face, rep = lax.axis_index("band"), lax.axis_index("face"), lax.axis_index("rep")
    me = band * faces + face

    sources = (w0, w1, w2, w3, w4, w5, w6, w7, w8)
    loads = [pltpu.make_async_copy(source, w_v.at[i], load_sem.at[i]) for i, source in enumerate(sources)]
    grid_load = pltpu.make_async_copy(grid_hbm, grid_v, load_sem.at[9])
    mesh_load = pltpu.make_async_copy(mesh_hbm, mesh_v, load_sem.at[10])
    grid_load.start()
    loads[0].start()
    mesh_load.start()
    for load in loads[1:]:
        load.start()

    def peer_id(step):
        other = lax.rem(me + step, peers)
        return {"band": other // faces, "face": other % faces}

    def each_peer(body):
        if peers <= 16:
            for step in range(1, peers):
                body(step)
        else:
            pl.loop(1, peers)(body)

    barrier = pltpu.get_barrier_semaphore()
    each_peer(
        lambda step: pl.semaphore_signal(
            barrier, inc=1, device_id=peer_id(step), device_id_type=pl.DeviceIdType.MESH
        )
    )

    mesh_row = own
    low_row = own + nodes
    high_row = low_row + rim
    geom_row = high_row + rim
    end_row = table.shape[0]

    grid_load.wait()
    loads[GRID_SEND].wait()
    table[pl.ds(0, own), :] = dot(grid_v[...], w_v[GRID_SEND]).astype(BF)

    pl.semaphore_wait(barrier, peers - 1)

    def rim_copy(source_row, target_row, target_band, which):
        return pltpu.make_async_remote_copy(
            src_ref=table.at[pl.ds(source_row, rim)],
            dst_ref=table.at[pl.ds(target_row, rim)],
            send_sem=halo_send.at[which],
            recv_sem=halo_recv.at[which],
            device_id={"band": target_band},
            device_id_type=pl.DeviceIdType.MESH,
        )

    up = rim_copy(own - rim, low_row, lax.rem(band + 1, bands), 0)
    down = rim_copy(0, high_row, lax.rem(band + bands - 1, bands), 1)
    has_up, has_down = band < bands - 1, band > 0

    @pl.when(has_up)
    def _():
        up.start()

    @pl.when(has_down)
    def _():
        down.start()

    @pl.when(band == 0)
    def _():
        table[pl.ds(low_row, rim), :] = jnp.zeros((rim, width), BF)

    @pl.when(band == bands - 1)
    def _():
        table[pl.ds(high_row, rim), :] = jnp.zeros((rim, width), BF)

    base = (band * lat_rows - RIM) * full_lon + (face * reps + rep) * lon_cols
    sender = g2m_sender[...] - base
    for lat in range(lat_rows + 2 * RIM):
        if lat < RIM:
            row = low_row + lat * lon_cols
        elif lat < RIM + lat_rows:
            row = (lat - RIM) * lon_cols
        else:
            row = high_row + (lat - RIM - lat_rows) * lon_cols
        hot_g[pl.ds(row, lon_cols), :] = hot(sender - lat * full_lon, lon_cols)
    live = lax.broadcasted_iota(jnp.int32, (1, g_edges), 1) < g2m_count[0]
    hot_g[pl.ds(mesh_row, nodes), :] = hot(jnp.where(live, g2m_receiver[...], -1), nodes)
    hot_g[pl.ds(geom_row, end_row - geom_row), :] = jnp.zeros((end_row - geom_row, g_edges), BF)
    hot_g[pl.ds(geom_row, 4), :] = g2m_geom[...]
    table[pl.ds(geom_row, end_row - geom_row), :] = jnp.zeros((end_row - geom_row, width), BF)
    table[pl.ds(geom_row, 4), :] = wgg[...]

    mesh_load.wait()
    loads[MESH_RECV].wait()
    table[pl.ds(mesh_row, nodes), :] = dot(mesh_v[...], w_v[MESH_RECV]).astype(BF)
    table_t[:, pl.ds(0, low_row)] = table[pl.ds(0, low_row), :].T
    loads[G2M_OUT].wait()
    out_t[...] = w_v[G2M_OUT].T
    loads[NODE_MESH].wait()
    node_input = dot(mesh_v[...], w_v[NODE_MESH])

    @pl.when(has_up)
    def _():
        up.wait_send()
        down.wait_recv()

    @pl.when(has_down)
    def _():
        down.wait_send()
        up.wait_recv()

    table_t[:, pl.ds(low_row, end_row - low_row)] = table[pl.ds(low_row, end_row - low_row), :].T

    g2m_sum = edge_sum(table_t, out_t, hot_g, mesh_row, nodes, g_edges)
    g2m_sum = (g2m_sum * g2m_gain[...]).astype(BF)

    loads[NODE_AGG].wait()
    node_hidden = silu(node_input + dot(g2m_sum, w_v[NODE_AGG])).astype(BF)
    loads[NODE_OUT].wait()
    update = normalized(dot(node_hidden, w_v[NODE_OUT]), 1) * node_gain[...]
    encoded = (mesh_v[...].astype(F32) + update).astype(BF)
    enc_out[...] = encoded

    chosen = dot(hot(send_rows[...], nodes), encoded, ((0,), (0,))).astype(BF)
    loads[PROC_SEND].wait()
    sent = dot(chosen, w_v[PROC_SEND]).astype(BF).astype(F32)
    for chunk in range(chunks):
        send_buf[pl.ds(chunk, listed, stride=chunks), :] = sent[:, chunk * LANES:(chunk + 1) * LANES]

    def row_copy(step):
        other = lax.rem(me + step, peers)
        return pltpu.make_async_remote_copy(
            src_ref=send_buf.at[pl.ds(pl.multiple_of(other * slot_rows, 8), slot_rows)],
            dst_ref=recv_buf.at[pl.ds(pl.multiple_of(me * slot_rows, 8), slot_rows)],
            send_sem=row_send.at[step],
            recv_sem=row_recv.at[step],
            device_id=peer_id(step),
            device_id_type=pl.DeviceIdType.MESH,
        )

    each_peer(lambda step: row_copy(step).start())
    mine = pl.ds(pl.multiple_of(me * slot_rows, 8), slot_rows)
    recv_buf[mine, :] = send_buf[mine, :]

    geom_m = listed + nodes
    end_m = table_m.shape[0]
    hot_m[pl.ds(0, listed), :] = hot(mesh_slot[...], listed)
    live = lax.broadcasted_iota(jnp.int32, (1, m_edges), 1) < mesh_count[0]
    hot_m[pl.ds(listed, nodes), :] = hot(jnp.where(live, mesh_receiver[...], -1), nodes)
    hot_m[pl.ds(geom_m, end_m - geom_m), :] = jnp.zeros((end_m - geom_m, m_edges), BF)
    hot_m[pl.ds(geom_m, 4), :] = mesh_geom[...]
    table_m[pl.ds(geom_m, end_m - geom_m), :] = jnp.zeros((end_m - geom_m, width), BF)
    table_m[pl.ds(geom_m, 4), :] = wpg[...]
    loads[PROC_RECV].wait()
    table_m[pl.ds(listed, nodes), :] = dot(encoded, w_v[PROC_RECV]).astype(BF)
    loads[PROC_OUT].wait()
    out_mt[...] = w_v[PROC_OUT].T

    each_peer(lambda step: row_copy(step).wait())
    for chunk in range(chunks):
        table_m[pl.ds(0, listed), pl.ds(chunk * LANES, LANES)] = recv_buf[
            pl.ds(chunk, listed, stride=chunks), :
        ].astype(BF)
    table_mt[...] = table_m[...].T
    messages = edge_sum(table_mt, out_mt, hot_m, listed, nodes, m_edges)
    msg_out[...] = (messages * proc_gain[...]).astype(BF)


def round_up(value, step):
    return (value + step - 1) // step * step


def on_device(
    bands,
    faces,
    reps,
    grid_latent,
    mesh_latent,
    w_grid_send,
    w_mesh_recv,
    w_g2m_geom,
    w_g2m_out,
    g2m_gain,
    w_node_mesh,
    w_node_agg,
    w_node_out,
    node_gain,
    w_proc_send,
    w_proc_recv,
    w_proc_geom,
    w_proc_out,
    proc_gain,
    g2m_sender,
    g2m_receiver,
    g2m_geom,
    g2m_count,
    mesh_receiver,
    mesh_slot,
    send_rows,
    mesh_geom,
    mesh_count,
):
    lat_rows, lon_cols, width = grid_latent.shape
    nodes = mesh_latent.shape[0]
    own = lat_rows * lon_cols
    g_edges, m_edges = g2m_sender.shape[0], mesh_slot.shape[0]
    peers = bands * faces
    listed = send_rows.shape[0]
    full_lon = lon_cols * faces * reps
    g_rows = round_up(own + nodes + 2 * RIM * lon_cols + 4, LANES)
    m_rows = round_up(listed + nodes + 4, LANES)
    row = lambda array: array.reshape(1, array.shape[0])
    hbm, vmem, smem = (pl.BlockSpec(memory_space=space) for space in (pl.ANY, pltpu.VMEM, pltpu.SMEM))
    rows_out = jax.ShapeDtypeStruct((nodes, width), BF)
    row_tiles = listed * width // LANES
    return pl.pallas_call(
        functools.partial(kernel, (bands, faces, reps, lat_rows, lon_cols, full_lon)),
        out_shape=(rows_out, rows_out),
        in_specs=[hbm] * 11 + [vmem] * 12 + [smem] * 2,
        out_specs=(vmem, vmem),
        scratch_shapes=[
            pltpu.VMEM((own, width), BF),
            pltpu.VMEM((nodes, width), BF),
            pltpu.VMEM((9, width, width), BF),
            pltpu.VMEM((g_rows, width), BF),
            pltpu.VMEM((width, g_rows), BF),
            pltpu.VMEM((width, width), BF),
            pltpu.VMEM((g_rows, g_edges), BF),
            pltpu.VMEM((m_rows, m_edges), BF),
            pltpu.VMEM((m_rows, width), BF),
            pltpu.VMEM((width, m_rows), BF),
            pltpu.VMEM((width, width), BF),
            pltpu.VMEM((row_tiles, LANES), F32),
            pltpu.VMEM((row_tiles, LANES), F32),
            pltpu.SemaphoreType.DMA((11,)),
            pltpu.SemaphoreType.DMA((2,)),
            pltpu.SemaphoreType.DMA((2,)),
            pltpu.SemaphoreType.DMA((peers,)),
            pltpu.SemaphoreType.DMA((peers,)),
        ],
        compiler_params=pltpu.CompilerParams(
            collective_id=0, has_side_effects=True, vmem_limit_bytes=48 * 1024 * 1024
        ),
        name="encode_and_edges",
    )(
        grid_latent.reshape(own, width), mesh_latent,
        w_grid_send, w_mesh_recv, w_g2m_out, w_node_mesh, w_node_agg, w_node_out, w_proc_send, w_proc_recv, w_proc_out,
        w_g2m_geom, w_proc_geom, row(g2m_gain), row(node_gain), row(proc_gain),
        row(g2m_sender), row(g2m_receiver), g2m_geom, row(mesh_receiver), row(mesh_slot), row(send_rows), mesh_geom,
        g2m_count, mesh_count,
    )


def solution(mesh):
    blocks = P(("member", "band", "face", "rep"), None)
    edges = P(("band", "face", "rep"))
    placed = (
        (P(("member", "band"), ("face", "rep"), None), blocks)
        + (P(),) * 14
        + (edges, edges, P(None, ("band", "face", "rep")), edges, edges, edges, edges)
        + (P(None, ("band", "face", "rep")), edges)
    )
    return jax.shard_map(
        functools.partial(on_device, mesh.shape["band"], mesh.shape["face"], mesh.shape["rep"]),
        mesh=mesh,
        in_specs=placed,
        out_specs=(blocks, blocks),
        check_vma=False,
    )
```

```python
import functools

import jax
import jax.numpy as jnp
from jax import lax
from jax.experimental import pallas as pl
from jax.experimental.pallas import tpu as pltpu
from jax.sharding import PartitionSpec as P

RIM = 2
EPSILON = 1e-05
LANES = 128
TILE = 1024
SMALL = 14
BF = jnp.bfloat16
F32 = jnp.float32

GRID_SEND, MESH_RECV, G2M_OUT, NODE_MESH, NODE_AGG, NODE_OUT, PROC_SEND, PROC_RECV, PROC_OUT = range(9)


def dot(a, b, contract=((1,), (0,))):
    return lax.dot_general(a, b, (contract, ((), ())), preferred_element_type=F32)


def silu(v):
    half = 0.5 * v
    return half + half * jnp.tanh(half)


def normalized(y, axis):
    scale = 1.0 / y.shape[axis]
    center = y - jnp.sum(y, axis=axis, keepdims=True) * scale
    spread = jnp.sum(center * center, axis=axis, keepdims=True) * scale
    return center * lax.rsqrt(spread + EPSILON)


def hot(index_row, rows):
    edges = index_row.shape[1]
    return jnp.where(lax.broadcasted_iota(jnp.int32, (rows, edges), 0) == index_row, 1.0, 0.0).astype(BF)


def edge_sum(table_t, out_t, hot_ref, receiver_row, nodes, edges):
    total = None
    for start in range(0, edges, TILE):
        cols = pl.ds(start, TILE)
        hidden = silu(dot(table_t[...], hot_ref[:, cols])).astype(BF)
        message = normalized(dot(out_t[...], hidden), 0).astype(BF)
        part = dot(hot_ref[pl.ds(receiver_row, nodes), cols], message, ((1,), (1,)))
        total = part if total is None else total + part
    return total


def kernel(
    dims,
    grid_hbm, mesh_hbm, w0, w1, w2, w3, w4, w5, w6, w7, w8,
    *rest,
):
    small_hbm, outs, small_v, scratch = (
        rest[:SMALL], rest[SMALL:SMALL + 2], rest[SMALL + 2:2 * SMALL + 2], rest[2 * SMALL + 2:]
    )
    enc_out, msg_out = outs
    (
        wgg, wpg, g2m_gain, node_gain, proc_gain,
        g2m_sender, g2m_receiver, g2m_geom, mesh_receiver, mesh_slot, send_rows, mesh_geom,
        g2m_count, mesh_count,
    ) = small_v
    (
        grid_v, mesh_v, w_v, table, table_t, out_t, hot_g, hot_m, table_m, table_mt, out_mt, send_buf, recv_buf,
        load_sem, small_sem, halo_send, halo_recv, row_send, row_recv,
    ) = scratch
    bands, faces, reps, lat_rows, lon_cols, full_lon = dims
    own, width = grid_v.shape
    nodes = mesh_v.shape[0]
    rim = RIM * lon_cols
    g_edges, m_edges = hot_g.shape[1], hot_m.shape[1]
    listed = send_rows.shape[1]
    peers = bands * faces
    slot_rows = send_buf.shape[0] // peers
    chunks = width // LANES
    band, face, rep = lax.axis_index("band"), lax.axis_index("face"), lax.axis_index("rep")
    me = band * faces + face

    sources = (w0, w1, w2, w3, w4, w5, w6, w7, w8)
    loads = [pltpu.make_async_copy(source, w_v.at[i], load_sem.at[i]) for i, source in enumerate(sources)]
    grid_load = pltpu.make_async_copy(grid_hbm, grid_v, load_sem.at[9])
    mesh_load = pltpu.make_async_copy(mesh_hbm, mesh_v, load_sem.at[10])
    small_loads = [
        pltpu.make_async_copy(source, target, small_sem.at[i])
        for i, (source, target) in enumerate(zip(small_hbm, small_v))
    ]
    grid_load.start()
    loads[0].start()
    for load in small_loads:
        load.start()
    mesh_load.start()
    for load in loads[1:]:
        load.start()

    def peer_id(step):
        other = lax.rem(me + step, peers)
        return {"band": other // faces, "face": other % faces}

    def each_peer(body):
        if peers <= 16:
            for step in range(1, peers):
                body(step)
        else:
            pl.loop(1, peers)(body)

    barrier = pltpu.get_barrier_semaphore()
    each_peer(
        lambda step: pl.semaphore_signal(
            barrier, inc=1, device_id=peer_id(step), device_id_type=pl.DeviceIdType.MESH
        )
    )

    mesh_row = own
    low_row = own + nodes
    high_row = low_row + rim
    geom_row = high_row + rim
    end_row = table.shape[0]

    grid_load.wait()
    loads[GRID_SEND].wait()
    table[pl.ds(0, own), :] = dot(grid_v[...], w_v[GRID_SEND]).astype(BF)

    pl.semaphore_wait(barrier, peers - 1)

    def rim_copy(source_row, target_row, target_band, which):
        return pltpu.make_async_remote_copy(
            src_ref=table.at[pl.ds(source_row, rim)],
            dst_ref=table.at[pl.ds(target_row, rim)],
            send_sem=halo_send.at[which],
            recv_sem=halo_recv.at[which],
            device_id={"band": target_band},
            device_id_type=pl.DeviceIdType.MESH,
        )

    up = rim_copy(own - rim, low_row, lax.rem(band + 1, bands), 0)
    down = rim_copy(0, high_row, lax.rem(band + bands - 1, bands), 1)
    has_up, has_down = band < bands - 1, band > 0

    @pl.when(has_up)
    def _():
        up.start()

    @pl.when(has_down)
    def _():
        down.start()

    @pl.when(band == 0)
    def _():
        table[pl.ds(low_row, rim), :] = jnp.zeros((rim, width), BF)

    @pl.when(band == bands - 1)
    def _():
        table[pl.ds(high_row, rim), :] = jnp.zeros((rim, width), BF)

    for load in small_loads:
        load.wait()

    base = (band * lat_rows - RIM) * full_lon + (face * reps + rep) * lon_cols
    sender = g2m_sender[...] - base
    for lat in range(lat_rows + 2 * RIM):
        if lat < RIM:
            row = low_row + lat * lon_cols
        elif lat < RIM + lat_rows:
            row = (lat - RIM) * lon_cols
        else:
            row = high_row + (lat - RIM - lat_rows) * lon_cols
        hot_g[pl.ds(row, lon_cols), :] = hot(sender - lat * full_lon, lon_cols)
    live = lax.broadcasted_iota(jnp.int32, (1, g_edges), 1) < g2m_count[...]
    hot_g[pl.ds(mesh_row, nodes), :] = hot(jnp.where(live, g2m_receiver[...], -1), nodes)
    hot_g[pl.ds(geom_row, end_row - geom_row), :] = jnp.zeros((end_row - geom_row, g_edges), BF)
    hot_g[pl.ds(geom_row, 4), :] = g2m_geom[...]
    table[pl.ds(geom_row, end_row - geom_row), :] = jnp.zeros((end_row - geom_row, width), BF)
    table[pl.ds(geom_row, 4), :] = wgg[...]

    mesh_load.wait()
    loads[MESH_RECV].wait()
    table[pl.ds(mesh_row, nodes), :] = dot(mesh_v[...], w_v[MESH_RECV]).astype(BF)
    table_t[:, pl.ds(0, low_row)] = table[pl.ds(0, low_row), :].T
    loads[G2M_OUT].wait()
    out_t[...] = w_v[G2M_OUT].T
    loads[NODE_MESH].wait()
    node_input = dot(mesh_v[...], w_v[NODE_MESH])

    @pl.when(has_up)
    def _():
        up.wait_send()
        down.wait_recv()

    @pl.when(has_down)
    def _():
        down.wait_send()
        up.wait_recv()

    table_t[:, pl.ds(low_row, end_row - low_row)] = table[pl.ds(low_row, end_row - low_row), :].T

    g2m_sum = edge_sum(table_t, out_t, hot_g, mesh_row, nodes, g_edges)
    g2m_sum = (g2m_sum * g2m_gain[...]).astype(BF)

    loads[NODE_AGG].wait()
    node_hidden = silu(node_input + dot(g2m_sum, w_v[NODE_AGG])).astype(BF)
    loads[NODE_OUT].wait()
    update = normalized(dot(node_hidden, w_v[NODE_OUT]), 1) * node_gain[...]
    encoded = (mesh_v[...].astype(F32) + update).astype(BF)
    enc_out[...] = encoded

    chosen = dot(hot(send_rows[...], nodes), encoded, ((0,), (0,))).astype(BF)
    loads[PROC_SEND].wait()
    sent = dot(chosen, w_v[PROC_SEND]).astype(BF).astype(F32)
    for chunk in range(chunks):
        send_buf[pl.ds(chunk, listed, stride=chunks), :] = sent[:, chunk * LANES:(chunk + 1) * LANES]

    def row_copy(step):
        other = lax.rem(me + step, peers)
        return pltpu.make_async_remote_copy(
            src_ref=send_buf.at[pl.ds(pl.multiple_of(other * slot_rows, 8), slot_rows)],
            dst_ref=recv_buf.at[pl.ds(pl.multiple_of(me * slot_rows, 8), slot_rows)],
            send_sem=row_send.at[step],
            recv_sem=row_recv.at[step],
            device_id=peer_id(step),
            device_id_type=pl.DeviceIdType.MESH,
        )

    each_peer(lambda step: row_copy(step).start())
    mine = pl.ds(pl.multiple_of(me * slot_rows, 8), slot_rows)
    recv_buf[mine, :] = send_buf[mine, :]

    geom_m = listed + nodes
    end_m = table_m.shape[0]
    hot_m[pl.ds(0, listed), :] = hot(mesh_slot[...], listed)
    live = lax.broadcasted_iota(jnp.int32, (1, m_edges), 1) < mesh_count[...]
    hot_m[pl.ds(listed, nodes), :] = hot(jnp.where(live, mesh_receiver[...], -1), nodes)
    hot_m[pl.ds(geom_m, end_m - geom_m), :] = jnp.zeros((end_m - geom_m, m_edges), BF)
    hot_m[pl.ds(geom_m, 4), :] = mesh_geom[...]
    table_m[pl.ds(geom_m, end_m - geom_m), :] = jnp.zeros((end_m - geom_m, width), BF)
    table_m[pl.ds(geom_m, 4), :] = wpg[...]
    loads[PROC_RECV].wait()
    table_m[pl.ds(listed, nodes), :] = dot(encoded, w_v[PROC_RECV]).astype(BF)
    loads[PROC_OUT].wait()
    out_mt[...] = w_v[PROC_OUT].T

    each_peer(lambda step: row_copy(step).wait())
    for chunk in range(chunks):
        table_m[pl.ds(0, listed), pl.ds(chunk * LANES, LANES)] = recv_buf[
            pl.ds(chunk, listed, stride=chunks), :
        ].astype(BF)
    table_mt[...] = table_m[...].T
    messages = edge_sum(table_mt, out_mt, hot_m, listed, nodes, m_edges)
    msg_out[...] = (messages * proc_gain[...]).astype(BF)


def hand_over(enc_in, msg_in, enc_out, msg_out, sems):
    copies = [
        pltpu.make_async_copy(source, target, sems.at[i])
        for i, (source, target) in enumerate(((enc_in, enc_out), (msg_in, msg_out)))
    ]
    for copy in copies:
        copy.start()
    for copy in copies:
        copy.wait()


def round_up(value, step):
    return (value + step - 1) // step * step


def on_device(
    bands,
    faces,
    reps,
    grid_latent,
    mesh_latent,
    w_grid_send,
    w_mesh_recv,
    w_g2m_geom,
    w_g2m_out,
    g2m_gain,
    w_node_mesh,
    w_node_agg,
    w_node_out,
    node_gain,
    w_proc_send,
    w_proc_recv,
    w_proc_geom,
    w_proc_out,
    proc_gain,
    g2m_sender,
    g2m_receiver,
    g2m_geom,
    g2m_count,
    mesh_receiver,
    mesh_slot,
    send_rows,
    mesh_geom,
    mesh_count,
):
    lat_rows, lon_cols, width = grid_latent.shape
    nodes = mesh_latent.shape[0]
    own = lat_rows * lon_cols
    g_edges, m_edges = g2m_sender.shape[0], mesh_slot.shape[0]
    peers = bands * faces
    listed = send_rows.shape[0]
    full_lon = lon_cols * faces * reps
    g_rows = round_up(own + nodes + 2 * RIM * lon_cols + 4, LANES)
    m_rows = round_up(listed + nodes + 4, LANES)
    row = lambda array: array.reshape(1, array.shape[0])
    hbm, vmem = (pl.BlockSpec(memory_space=space) for space in (pltpu.HBM, pltpu.VMEM))
    small = (
        w_g2m_geom, w_proc_geom, row(g2m_gain), row(node_gain), row(proc_gain),
        row(g2m_sender), row(g2m_receiver), g2m_geom, row(mesh_receiver), row(mesh_slot), row(send_rows), mesh_geom,
        row(g2m_count), row(mesh_count),
    )
    rows_out = jax.ShapeDtypeStruct((nodes, width), BF)
    row_tiles = listed * width // LANES
    held = pl.pallas_call(
        functools.partial(kernel, (bands, faces, reps, lat_rows, lon_cols, full_lon)),
        out_shape=(rows_out, rows_out),
        in_specs=[hbm] * (11 + SMALL),
        out_specs=(vmem, vmem),
        scratch_shapes=[
            *(pltpu.VMEM(array.shape, array.dtype) for array in small),
            pltpu.VMEM((own, width), BF),
            pltpu.VMEM((nodes, width), BF),
            pltpu.VMEM((9, width, width), BF),
            pltpu.VMEM((g_rows, width), BF),
            pltpu.VMEM((width, g_rows), BF),
            pltpu.VMEM((width, width), BF),
            pltpu.VMEM((g_rows, g_edges), BF),
            pltpu.VMEM((m_rows, m_edges), BF),
            pltpu.VMEM((m_rows, width), BF),
            pltpu.VMEM((width, m_rows), BF),
            pltpu.VMEM((width, width), BF),
            pltpu.VMEM((row_tiles, LANES), F32),
            pltpu.VMEM((row_tiles, LANES), F32),
            pltpu.SemaphoreType.DMA((11,)),
            pltpu.SemaphoreType.DMA((SMALL,)),
            pltpu.SemaphoreType.DMA((2,)),
            pltpu.SemaphoreType.DMA((2,)),
            pltpu.SemaphoreType.DMA((peers,)),
            pltpu.SemaphoreType.DMA((peers,)),
        ],
        compiler_params=pltpu.CompilerParams(
            collective_id=0, has_side_effects=True, vmem_limit_bytes=56 * 1024 * 1024
        ),
        name="encode_and_edges",
    )(
        grid_latent.reshape(own, width), mesh_latent,
        w_grid_send, w_mesh_recv, w_g2m_out, w_node_mesh, w_node_agg, w_node_out, w_proc_send, w_proc_recv, w_proc_out,
        *small,
    )
    return pl.pallas_call(
        hand_over,
        out_shape=(rows_out, rows_out),
        in_specs=[vmem, vmem],
        out_specs=(hbm, hbm),
        scratch_shapes=[pltpu.SemaphoreType.DMA((2,))],
        name="hand_over",
    )(*held)


def solution(mesh):
    blocks = P(("member", "band", "face", "rep"), None)
    edges = P(("band", "face", "rep"))
    placed = (
        (P(("member", "band"), ("face", "rep"), None), blocks)
        + (P(),) * 14
        + (edges, edges, P(None, ("band", "face", "rep")), edges, edges, edges, edges)
        + (P(None, ("band", "face", "rep")), edges)
    )
    return jax.shard_map(
        functools.partial(on_device, mesh.shape["band"], mesh.shape["face"], mesh.shape["rep"]),
        mesh=mesh,
        in_specs=placed,
        out_specs=(blocks, blocks),
        check_vma=False,
    )
```

```python
import functools

import jax
import jax.numpy as jnp
from jax import lax
from jax.experimental import pallas as pl
from jax.experimental.pallas import tpu as pltpu
from jax.sharding import PartitionSpec as P

RIM = 2
EPSILON = 1e-05
LANES = 128
TILE = 1024
SMALL = 14
BF = jnp.bfloat16
F32 = jnp.float32

GRID_SEND, MESH_RECV, G2M_OUT, NODE_MESH, NODE_AGG, NODE_OUT, PROC_SEND, PROC_RECV, PROC_OUT = range(9)


def dot(a, b, contract=((1,), (0,))):
    return lax.dot_general(a, b, (contract, ((), ())), preferred_element_type=F32)


def silu(v):
    half = 0.5 * v
    return half + half * jnp.tanh(half)


def normalized(y, axis):
    scale = 1.0 / y.shape[axis]
    center = y - jnp.sum(y, axis=axis, keepdims=True) * scale
    spread = jnp.sum(center * center, axis=axis, keepdims=True) * scale
    return center * lax.rsqrt(spread + EPSILON)


def hot(index_row, rows):
    edges = index_row.shape[1]
    return jnp.where(lax.broadcasted_iota(jnp.int32, (rows, edges), 0) == index_row, 1.0, 0.0).astype(BF)


def edge_sum(table_t, out_t, hot_ref, receiver_row, nodes, edges, early=None, first=0):
    total = None
    for start in range(0, edges, TILE):
        cols = pl.ds(start, TILE)
        rest = pl.ds(first, hot_ref.shape[0] - first)
        mixed = dot(table_t[:, rest], hot_ref[rest, cols])
        hidden = silu(mixed if early is None else mixed + early[:, cols]).astype(BF)
        message = normalized(dot(out_t[...], hidden), 0).astype(BF)
        part = dot(hot_ref[pl.ds(receiver_row, nodes), cols], message, ((1,), (1,)))
        total = part if total is None else total + part
    return total


def kernel(
    dims,
    grid_hbm, mesh_hbm, w0, w1, w2, w3, w4, w5, w6, w7, w8,
    *rest,
):
    small_hbm, outs, small_v, scratch = (
        rest[:SMALL], rest[SMALL:SMALL + 2], rest[SMALL + 2:2 * SMALL + 2], rest[2 * SMALL + 2:]
    )
    enc_out, msg_out = outs
    (
        wgg, wpg, g2m_gain, node_gain, proc_gain,
        g2m_sender, g2m_receiver, g2m_geom, mesh_receiver, mesh_slot, send_rows, mesh_geom,
        g2m_count, mesh_count,
    ) = small_v
    (
        grid_v, early, mesh_v, w_v, table, table_t, out_t, hot_g, hot_m, table_m, table_mt, out_mt, send_buf, recv_buf,
        load_sem, small_sem, halo_send, halo_recv, row_send, row_recv,
    ) = scratch
    bands, faces, reps, lat_rows, lon_cols, full_lon = dims
    own, width = grid_v.shape
    nodes = mesh_v.shape[0]
    rim = RIM * lon_cols
    g_edges, m_edges = hot_g.shape[1], hot_m.shape[1]
    listed = send_rows.shape[1]
    peers = bands * faces
    slot_rows = send_buf.shape[0] // peers
    chunks = width // LANES
    band, face, rep = lax.axis_index("band"), lax.axis_index("face"), lax.axis_index("rep")
    me = band * faces + face

    sources = (w0, w1, w2, w3, w4, w5, w6, w7, w8)
    loads = [pltpu.make_async_copy(source, w_v.at[i], load_sem.at[i]) for i, source in enumerate(sources)]
    grid_load = pltpu.make_async_copy(grid_hbm, grid_v, load_sem.at[9])
    mesh_load = pltpu.make_async_copy(mesh_hbm, mesh_v, load_sem.at[10])
    small_loads = [
        pltpu.make_async_copy(source, target, small_sem.at[i])
        for i, (source, target) in enumerate(zip(small_hbm, small_v))
    ]
    grid_load.start()
    loads[0].start()
    for load in small_loads:
        load.start()
    mesh_load.start()
    for load in loads[1:]:
        load.start()

    def peer_id(step):
        other = lax.rem(me + step, peers)
        return {"band": other // faces, "face": other % faces}

    def each_peer(body):
        if peers <= 16:
            for step in range(1, peers):
                body(step)
        else:
            pl.loop(1, peers)(body)

    barrier = pltpu.get_barrier_semaphore()
    each_peer(
        lambda step: pl.semaphore_signal(
            barrier, inc=1, device_id=peer_id(step), device_id_type=pl.DeviceIdType.MESH
        )
    )

    mesh_row = own
    low_row = own + nodes
    high_row = low_row + rim
    geom_row = high_row + rim
    end_row = table.shape[0]

    grid_load.wait()
    loads[GRID_SEND].wait()
    table[pl.ds(0, own), :] = dot(grid_v[...], w_v[GRID_SEND]).astype(BF)

    pl.semaphore_wait(barrier, peers - 1)

    def rim_copy(source_row, target_row, target_band, which):
        return pltpu.make_async_remote_copy(
            src_ref=table.at[pl.ds(source_row, rim)],
            dst_ref=table.at[pl.ds(target_row, rim)],
            send_sem=halo_send.at[which],
            recv_sem=halo_recv.at[which],
            device_id={"band": target_band},
            device_id_type=pl.DeviceIdType.MESH,
        )

    up = rim_copy(own - rim, low_row, lax.rem(band + 1, bands), 0)
    down = rim_copy(0, high_row, lax.rem(band + bands - 1, bands), 1)
    has_up, has_down = band < bands - 1, band > 0

    @pl.when(has_up)
    def _():
        up.start()

    @pl.when(has_down)
    def _():
        down.start()

    @pl.when(band == 0)
    def _():
        table[pl.ds(low_row, rim), :] = jnp.zeros((rim, width), BF)

    @pl.when(band == bands - 1)
    def _():
        table[pl.ds(high_row, rim), :] = jnp.zeros((rim, width), BF)

    for load in small_loads:
        load.wait()

    base = (band * lat_rows - RIM) * full_lon + (face * reps + rep) * lon_cols
    sender = g2m_sender[...] - base
    for lat in range(lat_rows + 2 * RIM):
        if lat < RIM:
            row = low_row + lat * lon_cols
        elif lat < RIM + lat_rows:
            row = (lat - RIM) * lon_cols
        else:
            row = high_row + (lat - RIM - lat_rows) * lon_cols
        hot_g[pl.ds(row, lon_cols), :] = hot(sender - lat * full_lon, lon_cols)
    live = lax.broadcasted_iota(jnp.int32, (1, g_edges), 1) < g2m_count[...]
    hot_g[pl.ds(mesh_row, nodes), :] = hot(jnp.where(live, g2m_receiver[...], -1), nodes)
    hot_g[pl.ds(geom_row, end_row - geom_row), :] = jnp.zeros((end_row - geom_row, g_edges), BF)
    hot_g[pl.ds(geom_row, 4), :] = g2m_geom[...]
    table[pl.ds(geom_row, end_row - geom_row), :] = jnp.zeros((end_row - geom_row, width), BF)
    table[pl.ds(geom_row, 4), :] = wgg[...]

    mesh_load.wait()
    loads[MESH_RECV].wait()
    table[pl.ds(mesh_row, nodes), :] = dot(mesh_v[...], w_v[MESH_RECV]).astype(BF)
    table_t[:, pl.ds(0, low_row)] = table[pl.ds(0, low_row), :].T
    loads[G2M_OUT].wait()
    out_t[...] = w_v[G2M_OUT].T
    loads[NODE_MESH].wait()
    node_input = dot(mesh_v[...], w_v[NODE_MESH])
    for start in range(0, g_edges, TILE):
        cols = pl.ds(start, TILE)
        early[:, cols] = dot(table_t[:, pl.ds(0, low_row)], hot_g[pl.ds(0, low_row), cols])

    @pl.when(has_up)
    def _():
        up.wait_send()
        down.wait_recv()

    @pl.when(has_down)
    def _():
        down.wait_send()
        up.wait_recv()

    table_t[:, pl.ds(low_row, end_row - low_row)] = table[pl.ds(low_row, end_row - low_row), :].T

    g2m_sum = edge_sum(table_t, out_t, hot_g, mesh_row, nodes, g_edges, early, low_row)
    g2m_sum = (g2m_sum * g2m_gain[...]).astype(BF)

    loads[NODE_AGG].wait()
    node_hidden = silu(node_input + dot(g2m_sum, w_v[NODE_AGG])).astype(BF)
    loads[NODE_OUT].wait()
    update = normalized(dot(node_hidden, w_v[NODE_OUT]), 1) * node_gain[...]
    encoded = (mesh_v[...].astype(F32) + update).astype(BF)
    enc_out[...] = encoded

    chosen = dot(hot(send_rows[...], nodes), encoded, ((0,), (0,))).astype(BF)
    loads[PROC_SEND].wait()
    sent = dot(chosen, w_v[PROC_SEND]).astype(BF).astype(F32)
    for chunk in range(chunks):
        send_buf[pl.ds(chunk, listed, stride=chunks), :] = sent[:, chunk * LANES:(chunk + 1) * LANES]

    def row_copy(step):
        other = lax.rem(me + step, peers)
        return pltpu.make_async_remote_copy(
            src_ref=send_buf.at[pl.ds(pl.multiple_of(other * slot_rows, 8), slot_rows)],
            dst_ref=recv_buf.at[pl.ds(pl.multiple_of(me * slot_rows, 8), slot_rows)],
            send_sem=row_send.at[step],
            recv_sem=row_recv.at[step],
            device_id=peer_id(step),
            device_id_type=pl.DeviceIdType.MESH,
        )

    each_peer(lambda step: row_copy(step).start())
    mine = pl.ds(pl.multiple_of(me * slot_rows, 8), slot_rows)
    recv_buf[mine, :] = send_buf[mine, :]

    geom_m = listed + nodes
    end_m = table_m.shape[0]
    hot_m[pl.ds(0, listed), :] = hot(mesh_slot[...], listed)
    live = lax.broadcasted_iota(jnp.int32, (1, m_edges), 1) < mesh_count[...]
    hot_m[pl.ds(listed, nodes), :] = hot(jnp.where(live, mesh_receiver[...], -1), nodes)
    hot_m[pl.ds(geom_m, end_m - geom_m), :] = jnp.zeros((end_m - geom_m, m_edges), BF)
    hot_m[pl.ds(geom_m, 4), :] = mesh_geom[...]
    table_m[pl.ds(geom_m, end_m - geom_m), :] = jnp.zeros((end_m - geom_m, width), BF)
    table_m[pl.ds(geom_m, 4), :] = wpg[...]
    loads[PROC_RECV].wait()
    table_m[pl.ds(listed, nodes), :] = dot(encoded, w_v[PROC_RECV]).astype(BF)
    loads[PROC_OUT].wait()
    out_mt[...] = w_v[PROC_OUT].T

    each_peer(lambda step: row_copy(step).wait())
    for chunk in range(chunks):
        table_m[pl.ds(0, listed), pl.ds(chunk * LANES, LANES)] = recv_buf[
            pl.ds(chunk, listed, stride=chunks), :
        ].astype(BF)
    table_mt[...] = table_m[...].T
    messages = edge_sum(table_mt, out_mt, hot_m, listed, nodes, m_edges)
    msg_out[...] = (messages * proc_gain[...]).astype(BF)


def hand_over(enc_in, msg_in, enc_out, msg_out, sems):
    copies = [
        pltpu.make_async_copy(source, target, sems.at[i])
        for i, (source, target) in enumerate(((enc_in, enc_out), (msg_in, msg_out)))
    ]
    for copy in copies:
        copy.start()
    for copy in copies:
        copy.wait()


def round_up(value, step):
    return (value + step - 1) // step * step


def on_device(
    bands,
    faces,
    reps,
    grid_latent,
    mesh_latent,
    w_grid_send,
    w_mesh_recv,
    w_g2m_geom,
    w_g2m_out,
    g2m_gain,
    w_node_mesh,
    w_node_agg,
    w_node_out,
    node_gain,
    w_proc_send,
    w_proc_recv,
    w_proc_geom,
    w_proc_out,
    proc_gain,
    g2m_sender,
    g2m_receiver,
    g2m_geom,
    g2m_count,
    mesh_receiver,
    mesh_slot,
    send_rows,
    mesh_geom,
    mesh_count,
):
    lat_rows, lon_cols, width = grid_latent.shape
    nodes = mesh_latent.shape[0]
    own = lat_rows * lon_cols
    g_edges, m_edges = g2m_sender.shape[0], mesh_slot.shape[0]
    peers = bands * faces
    listed = send_rows.shape[0]
    full_lon = lon_cols * faces * reps
    g_rows = round_up(own + nodes + 2 * RIM * lon_cols + 4, LANES)
    m_rows = round_up(listed + nodes + 4, LANES)
    row = lambda array: array.reshape(1, array.shape[0])
    hbm, vmem = (pl.BlockSpec(memory_space=space) for space in (pltpu.HBM, pltpu.VMEM))
    small = (
        w_g2m_geom, w_proc_geom, row(g2m_gain), row(node_gain), row(proc_gain),
        row(g2m_sender), row(g2m_receiver), g2m_geom, row(mesh_receiver), row(mesh_slot), row(send_rows), mesh_geom,
        row(g2m_count), row(mesh_count),
    )
    rows_out = jax.ShapeDtypeStruct((nodes, width), BF)
    row_tiles = listed * width // LANES
    held = pl.pallas_call(
        functools.partial(kernel, (bands, faces, reps, lat_rows, lon_cols, full_lon)),
        out_shape=(rows_out, rows_out),
        in_specs=[hbm] * (11 + SMALL),
        out_specs=(vmem, vmem),
        scratch_shapes=[
            *(pltpu.VMEM(array.shape, array.dtype) for array in small),
            pltpu.VMEM((own, width), BF),
            pltpu.VMEM((width, g_edges), F32),
            pltpu.VMEM((nodes, width), BF),
            pltpu.VMEM((9, width, width), BF),
            pltpu.VMEM((g_rows, width), BF),
            pltpu.VMEM((width, g_rows), BF),
            pltpu.VMEM((width, width), BF),
            pltpu.VMEM((g_rows, g_edges), BF),
            pltpu.VMEM((m_rows, m_edges), BF),
            pltpu.VMEM((m_rows, width), BF),
            pltpu.VMEM((width, m_rows), BF),
            pltpu.VMEM((width, width), BF),
            pltpu.VMEM((row_tiles, LANES), F32),
            pltpu.VMEM((row_tiles, LANES), F32),
            pltpu.SemaphoreType.DMA((11,)),
            pltpu.SemaphoreType.DMA((SMALL,)),
            pltpu.SemaphoreType.DMA((2,)),
            pltpu.SemaphoreType.DMA((2,)),
            pltpu.SemaphoreType.DMA((peers,)),
            pltpu.SemaphoreType.DMA((peers,)),
        ],
        compiler_params=pltpu.CompilerParams(
            collective_id=0, has_side_effects=True, vmem_limit_bytes=56 * 1024 * 1024
        ),
        name="encode_and_edges",
    )(
        grid_latent.reshape(own, width), mesh_latent,
        w_grid_send, w_mesh_recv, w_g2m_out, w_node_mesh, w_node_agg, w_node_out, w_proc_send, w_proc_recv, w_proc_out,
        *small,
    )
    return pl.pallas_call(
        hand_over,
        out_shape=(rows_out, rows_out),
        in_specs=[vmem, vmem],
        out_specs=(hbm, hbm),
        scratch_shapes=[pltpu.SemaphoreType.DMA((2,))],
        name="hand_over",
    )(*held)


def solution(mesh):
    blocks = P(("member", "band", "face", "rep"), None)
    edges = P(("band", "face", "rep"))
    placed = (
        (P(("member", "band"), ("face", "rep"), None), blocks)
        + (P(),) * 14
        + (edges, edges, P(None, ("band", "face", "rep")), edges, edges, edges, edges)
        + (P(None, ("band", "face", "rep")), edges)
    )
    return jax.shard_map(
        functools.partial(on_device, mesh.shape["band"], mesh.shape["face"], mesh.shape["rep"]),
        mesh=mesh,
        in_specs=placed,
        out_specs=(blocks, blocks),
        check_vma=False,
    )
```
